32 devices in a mesh: rows: 8 (over z, x), feat: 4 (over y, core).
Axes of the slice: x: 2, y: 2, z: 4, core: 2. Of those that a mesh axis runs over, the one named last changes fastest.
Arguments:
- samples: float32 [8192, 440], P(('rows', 'feat')), may hold values from -6 to 6
- residual: float32 [8192, 147], P(('rows', 'feat')), may hold values from -4 to 4
- projections: float32 [8, 440, 1024], P('feat'), may hold values from -0.4375 to 0.4375
- phases: float32 [8, 1024], P('feat'), may hold values from 0 to 6.2831855
- weights: float32 [8, 1024, 147], P('feat'), may hold values from -4 to 4
- block_order: int32 [8], replicated, may hold values from 0 to 7, each once
Outputs:
- residual_out: float32 [8192, 147], P(('rows', 'feat'))
- new_weights: float32 [1, 1024, 147], replicated
The draws below stay inside these ranges and needn't reach their ends.
Inputs may be any that keep to these rules, and one draw needn't show every extreme that they name: Block k is held by index k // 2 of feat; the blocks updated are those of the first 1 entries of block_order.
All inputs are finite; a program needn't handle non-finite values.
Results may differ from the reference program's by a relative error of at most 0.0003.
Values sent between devices are 32-bit elements; how exact they have to be, the bound alone decides.
A program may use at most 128 MiB of HBM per device.

```python
import jax
import jax.numpy as jnp
from jax import lax

D_IN = 440
BLK = 1024
OUT = 147
UPDATES = 1
BLOCKS = 8
TOTAL_ROWS = 8192


def shared_draw(key):
    inner = jax.random.fold_in(key, 7)
    first, second, third = jax.random.split(inner, 3)
    samples = jnp.clip(jax.random.normal(first, (TOTAL_ROWS, D_IN), jnp.float32), -6.0, 6.0)
    mixing = jax.random.normal(second, (D_IN, OUT), jnp.float32) / jnp.sqrt(jnp.float32(D_IN))
    signal = 1.5 * jnp.sin(jnp.dot(samples, mixing, precision=lax.Precision.HIGHEST))
    noise = 0.5 * jnp.clip(jax.random.normal(third, (TOTAL_ROWS, OUT), jnp.float32), -4.0, 4.0)
    residual = signal + noise
    return (samples, jnp.clip(residual, -4.0, 4.0))


def draw_samples(key, part):
    return shared_draw(key)[0]


def draw_residual(key, part):
    return shared_draw(key)[1]


def level_of(own_key, dims, cuts, smallest, top_value):
    level, own = 1.0, jax.random.fold_in(own_key, 6)
    for position, shards_of in cuts:
        heights = jnp.exp(jax.random.uniform(jax.random.fold_in(own, position), (shards_of,), jnp.float32, smallest / len(cuts), top_value / len(cuts)))
        level = level * jnp.repeat(heights, dims[position] // shards_of).reshape([-1 if axis == position else 1 for axis in range(len(dims))])
    return level


def scatter_about(key, shape, width, most, shards=(), held_as=jnp.bfloat16):
    array = jax.random.normal(key, shape, jnp.float32) * width
    if len(shards) > 0:
        array = level_of(key, shape, shards, -0.22, 0.18) * array
    return jnp.clip(array, min=-most, max=most).astype(held_as)


def setup_inputs(seed: int = 0) -> dict:
    arg_keys = jax.random.split(jax.random.key(seed), 7)
    return {
        "samples": draw_samples(jax.random.fold_in(arg_keys[6], 71), 0),
        "residual": draw_residual(jax.random.fold_in(arg_keys[6], 71), 0),
        "projections": scatter_about(arg_keys[2], (BLOCKS, D_IN, BLK), (D_IN // 2) ** -0.5, 0.4375, ((0, 4),), jnp.float32),
        "phases": jnp.clip(6.2831855 * jax.random.uniform(arg_keys[3], (BLOCKS, BLK), jnp.float32) ** level_of(arg_keys[3], (BLOCKS, BLK), ((0, 4),), -0.2, 0.2), 0.0, 6.2831855),
        "weights": scatter_about(arg_keys[4], (BLOCKS, BLK, OUT), 0.3, 4.0, ((0, 4),), jnp.float32),
        "block_order": jax.random.permutation(arg_keys[5], BLOCKS).astype(jnp.int32),
    }


root_two = 1.4142135623730951
penalty = 0.05

def features_of(samples, basis_block, phase_block):
    projected = jnp.dot(samples.astype(jnp.float32), basis_block.astype(jnp.float32), precision=lax.Precision.HIGHEST, preferred_element_type=jnp.float32)
    return root_two * jnp.cos(projected + phase_block)

def reference(samples, residual, projections, phases, weights, block_order):
    results = []
    for update in range(UPDATES):
        block_id = block_order[update].astype(jnp.int32)
        basis_block = lax.dynamic_index_in_dim(projections, block_id, 0, False)
        phase_block = lax.dynamic_index_in_dim(phases, block_id, 0, False)
        old_weights = lax.dynamic_index_in_dim(weights, block_id, 0, False)
        features = features_of(samples, basis_block, phase_block)
        gram_matrix = jnp.dot(features.T.astype(jnp.float32), features.astype(jnp.float32), precision=lax.Precision.HIGHEST, preferred_element_type=jnp.float32) / TOTAL_ROWS
        cross_term = jnp.dot(features.T.astype(jnp.float32), residual.astype(jnp.float32), precision=lax.Precision.HIGHEST, preferred_element_type=jnp.float32) / TOTAL_ROWS
        system = gram_matrix + penalty * jnp.eye(BLK, dtype=jnp.float32)
        factor = jnp.linalg.cholesky(system)
        change = jax.scipy.linalg.cho_solve((factor, True), cross_term - penalty * old_weights)
        results.append(old_weights + change)
        residual = residual - jnp.dot(features.astype(jnp.float32), change.astype(jnp.float32), precision=lax.Precision.HIGHEST, preferred_element_type=jnp.float32)
    return (residual, jnp.stack(results))
```

```python
import functools

import jax
import jax.numpy as jnp
from jax import lax
from jax.experimental import pallas as pl
from jax.experimental.pallas import tpu as pltpu
from jax.sharding import PartitionSpec as P

root_two = 1.4142135623730951
penalty = 0.05
LANES = 128
HIGHEST = lax.Precision.HIGHEST
VMEM_LIMIT = 48 * 1024 * 1024


def round_up(value, step):
    return -(-value // step) * step


def dot_nt(left, right):
    return lax.dot_general(
        left, right, (((1,), (1,)), ((), ())), precision=HIGHEST, preferred_element_type=jnp.float32
    )


def dot_nn(left, right):
    return lax.dot_general(
        left, right, (((1,), (0,)), ((), ())), precision=HIGHEST, preferred_element_type=jnp.float32
    )


def axis_bits(name, size):
    bits, step = [], 1
    while step < size:
        bits.append((name, step))
        step *= 2
    return bits


def greet(bits):
    barrier = pltpu.get_barrier_semaphore()
    for name, step in bits:
        me = lax.axis_index(name)
        partner = me + step * (1 - 2 * ((me // step) % 2))
        pl.semaphore_signal(
            barrier, inc=1, device_id={name: partner}, device_id_type=pl.DeviceIdType.MESH
        )
    pl.semaphore_wait(barrier, len(bits))


def sum_over(plans, buf, recv, out, send_sems, recv_sems):
    rows_of = lambda start, size: pl.ds(pl.multiple_of(start, 8), size)
    state = [(base, rows) for base, rows, _ in plans]
    landing = [base for base, _, _ in plans]
    count = len(plans[0][2])

    def peer(part, step):
        name, stride = plans[part][2][step]
        me = lax.axis_index(name)
        bit = (me // stride) % 2
        return name, me + stride * (1 - 2 * bit), bit

    for step in range(count):
        copies = []
        for part in range(len(plans)):
            name, partner, bit = peer(part, step)
            start, size = state[part]
            half = size // 2
            copy = pltpu.make_async_remote_copy(
                src_ref=buf.at[rows_of(start + (1 - bit) * half, half)],
                dst_ref=recv.at[pl.ds(landing[part], half)],
                send_sem=send_sems.at[0, part, step],
                recv_sem=recv_sems.at[0, part, step],
                device_id={name: partner},
                device_id_type=pl.DeviceIdType.MESH,
            )
            copy.start()
            copies.append(copy)
            state[part] = (start + bit * half, half)
        for part, copy in enumerate(copies):
            copy.wait()
            start, half = state[part]
            mine = rows_of(start, half)
            buf[mine, :] = buf[mine, :] + recv[pl.ds(landing[part], half), :]
            landing[part] += half
    for start, size in state:
        mine = rows_of(start, size)
        out[mine, :] = buf[mine, :]
    for step in reversed(range(count)):
        copies = []
        for part in range(len(plans)):
            name, partner, bit = peer(part, step)
            start, size = state[part]
            mine = rows_of(start, size)
            copy = pltpu.make_async_remote_copy(
                src_ref=out.at[mine],
                dst_ref=out.at[mine],
                send_sem=send_sems.at[1, part, step],
                recv_sem=recv_sems.at[1, part, step],
                device_id={name: partner},
                device_id_type=pl.DeviceIdType.MESH,
            )
            copy.start()
            copies.append(copy)
            state[part] = (start - bit * size, size * 2)
        for copy in copies:
            copy.wait()


def spread_kernel(bits, plans, block_ref, out_ref, buf, recv, send_sems, recv_sems):
    greet(bits)
    buf[...] = block_ref[...]
    sum_over(plans, buf, recv, out_ref, send_sems, recv_sems)


def gram_kernel(bits, plans, features_ref, targets_ref, out_ref, buf, recv, send_sems, recv_sems):
    greet(bits)
    tiles = features_ref.shape[0] // LANES
    at = 0
    for i in range(tiles):
        panel = dot_nt(features_ref[i * LANES:(i + 1) * LANES, :], features_ref[:(i + 1) * LANES, :])
        for j in range(i + 1):
            buf[at:at + LANES, :] = panel[:, j * LANES:(j + 1) * LANES]
            at += LANES
    cross = dot_nt(targets_ref[...], features_ref[...])
    depth = cross.shape[0]
    for j in range(tiles):
        buf[at:at + depth, :] = cross[:, j * LANES:(j + 1) * LANES]
        at += depth
    if at < buf.shape[0]:
        buf[at:, :] = jnp.zeros((buf.shape[0] - at, LANES), jnp.float32)
    sum_over(plans, buf, recv, out_ref, send_sems, recv_sems)


def summing_call(kernel, bits, orders, rows, operands, collective_id):
    part_rows = rows // len(orders)
    plans = [(n * part_rows, part_rows, order) for n, order in enumerate(orders)]
    sems = pltpu.SemaphoreType.DMA((2, len(orders), len(bits)))
    return pl.pallas_call(
        functools.partial(kernel, bits, plans),
        out_shape=jax.ShapeDtypeStruct((rows, LANES), jnp.float32),
        in_specs=[pl.BlockSpec(memory_space=pltpu.VMEM)] * len(operands),
        out_specs=pl.BlockSpec(memory_space=pltpu.VMEM),
        scratch_shapes=[
            pltpu.VMEM((rows, LANES), jnp.float32),
            pltpu.VMEM((rows, LANES), jnp.float32),
            sems,
            sems,
        ],
        compiler_params=pltpu.CompilerParams(
            collective_id=collective_id, has_side_effects=True, vmem_limit_bytes=VMEM_LIMIT
        ),
    )(*operands)


def invert(block):
    size = block.shape[0]
    pieces = [block[8 * n:8 * n + 8, :] for n in range(size // 8)]
    lane = lax.broadcasted_iota(jnp.int32, (1, size), 1)
    sub = lax.broadcasted_iota(jnp.int32, (8, 1), 0)
    for k in range(size):
        home, at = k // 8, k % 8
        row = pieces[home][at:at + 1, :]
        inverse = 1.0 / row[:, k:k + 1]
        scaled = row * inverse
        factor = jnp.where(lane == k, 1.0 + inverse, scaled)
        kept = jnp.where(lane == k, inverse, scaled)
        pieces = [piece - piece[:, k:k + 1] * factor for piece in pieces]
        pieces[home] = jnp.where(sub == at, kept, pieces[home])
    return jnp.concatenate(pieces, axis=0)


def solve_kernel(total_rows, packed_ref, weights_ref, change_ref, panels, diagonal_inverse):
    width = weights_ref.shape[1]
    depth = weights_ref.shape[0]
    tiles = width // LANES
    scale = 1.0 / total_rows
    eye = (
        lax.broadcasted_iota(jnp.int32, (LANES, LANES), 0)
        == lax.broadcasted_iota(jnp.int32, (LANES, LANES), 1)
    )
    at = 0
    for i in range(tiles):
        for j in range(i + 1):
            block = packed_ref[at:at + LANES, :] * scale
            if i == j:
                block = jnp.where(eye, block + penalty, block)
            panels[j, i * LANES:(i + 1) * LANES, :] = block
            at += LANES
    for j in range(tiles):
        panels[j, width:, :] = (
            packed_ref[at:at + depth, :] * scale - penalty * weights_ref[:, j * LANES:(j + 1) * LANES]
        )
        at += depth

    def eliminate(j):
        below = (j + 1) * LANES
        ratio = dot_nn(panels[j, below:, :], diagonal_inverse[...])
        for k in range(j + 1, tiles):
            panels[k, k * LANES:, :] = panels[k, k * LANES:, :] - dot_nt(
                ratio[(k - j - 1) * LANES:, :], panels[j, k * LANES:(k + 1) * LANES, :]
            )
        panels[j, below:, :] = ratio

    def step(j, carry):
        diagonal_inverse[...] = invert(panels[j, pl.ds(pl.multiple_of(j * LANES, LANES), LANES), :])
        for n in range(tiles):
            pl.when(j == n)(functools.partial(eliminate, n))
        return carry

    lax.fori_loop(0, tiles, step, 0)
    for j in reversed(range(tiles)):
        answer = panels[j, width:, :]
        if j + 1 < tiles:
            answer = answer - dot_nn(
                change_ref[:, (j + 1) * LANES:], panels[j, (j + 1) * LANES:width, :]
            )
        change_ref[:, j * LANES:(j + 1) * LANES] = answer


def body(samples, residual, projections, phases, weights, block_order):
    per_device, inputs, width = projections.shape
    classes = residual.shape[1]
    depth = round_up(classes, 8)
    feat_bits = axis_bits("feat", lax.axis_size("feat"))
    rows_bits = axis_bits("rows", lax.axis_size("rows"))
    total_rows = samples.shape[0] * lax.axis_size("rows") * lax.axis_size("feat")
    block_id = block_order[0]
    slot = block_id % per_device
    mine = lax.axis_index("feat") == block_id // per_device

    def local(array):
        block = lax.dynamic_index_in_dim(array, slot, 0, False)
        return jnp.where(mine, block, jnp.zeros_like(block))

    old_weights = lax.psum(local(weights), "feat")
    tiles = width // LANES
    spread_rows = round_up((inputs + 8) * tiles, 8 * 2 ** len(feat_bits))
    basis = jnp.concatenate(
        [local(projections), jnp.broadcast_to(local(phases)[None], (8, width))], axis=0
    ).reshape(-1, LANES)
    basis = jnp.pad(basis, ((0, spread_rows - basis.shape[0]), (0, 0)))
    spread = summing_call(spread_kernel, feat_bits, [feat_bits], spread_rows, [basis], 1)
    spread = spread[:(inputs + 8) * tiles].reshape(inputs + 8, width)
    projected = lax.dot_general(
        spread[:inputs], samples, (((0,), (1,)), ((), ())),
        precision=HIGHEST, preferred_element_type=jnp.float32,
    )
    features = root_two * jnp.cos(projected + spread[inputs][:, None])
    targets = jnp.pad(residual.T, ((0, depth - classes), (0, 0)))

    orders = [
        feat_bits + rows_bits,
        feat_bits[:1] + rows_bits[:1] + feat_bits[1:] + rows_bits[1:][::-1],
    ]
    bits = feat_bits + rows_bits
    sum_rows = round_up(
        tiles * (tiles + 1) // 2 * LANES + tiles * depth, 8 * 2 ** len(bits) * len(orders)
    )
    packed = summing_call(gram_kernel, bits, orders, sum_rows, [features, targets], 2)

    change = pl.pallas_call(
        functools.partial(solve_kernel, total_rows),
        out_shape=jax.ShapeDtypeStruct((depth, width), jnp.float32),
        in_specs=[pl.BlockSpec(memory_space=pltpu.VMEM)] * 2,
        out_specs=pl.BlockSpec(memory_space=pltpu.VMEM),
        scratch_shapes=[
            pltpu.VMEM((tiles, width + depth, LANES), jnp.float32),
            pltpu.VMEM((LANES, LANES), jnp.float32),
        ],
        compiler_params=pltpu.CompilerParams(vmem_limit_bytes=VMEM_LIMIT),
    )(packed, jnp.pad(old_weights.T, ((0, depth - classes), (0, 0))))[:classes]

    new_weights = old_weights + change.T
    taken = lax.dot_general(
        change, features, (((1,), (0,)), ((), ())), precision=HIGHEST, preferred_element_type=jnp.float32
    )
    return residual - taken.T, new_weights[None]


def solution(mesh):
    return jax.shard_map(
        body,
        mesh=mesh,
        in_specs=(
            P(("rows", "feat"), None),
            P(("rows", "feat"), None),
            P("feat", None, None),
            P("feat", None),
            P("feat", None, None),
            P(),
        ),
        out_specs=(P(("rows", "feat"), None), P()),
        check_vma=False,
    )
```

```python
import functools

import jax
import jax.numpy as jnp
from jax import lax
from jax.experimental import pallas as pl
from jax.experimental.pallas import tpu as pltpu
from jax.sharding import PartitionSpec as P

root_two = 1.4142135623730951
penalty = 0.05
LANES = 128
HIGHEST = lax.Precision.HIGHEST
VMEM_LIMIT = 48 * 1024 * 1024


def round_up(value, step):
    return -(-value // step) * step


def dot_nt(left, right):
    return lax.dot_general(
        left, right, (((1,), (1,)), ((), ())), precision=HIGHEST, preferred_element_type=jnp.float32
    )


def dot_nn(left, right):
    return lax.dot_general(
        left, right, (((1,), (0,)), ((), ())), precision=HIGHEST, preferred_element_type=jnp.float32
    )


def axis_bits(name, size):
    bits, step = [], 1
    while step < size:
        bits.append((name, step))
        step *= 2
    return bits


def greet(bits):
    barrier = pltpu.get_barrier_semaphore()
    for name, step in bits:
        me = lax.axis_index(name)
        partner = me + step * (1 - 2 * ((me // step) % 2))
        pl.semaphore_signal(
            barrier, inc=1, device_id={name: partner}, device_id_type=pl.DeviceIdType.MESH
        )
    pl.semaphore_wait(barrier, len(bits))


def sum_over(plans, buf, recv, out, send_sems, recv_sems, alike=()):
    rows_of = lambda start, size: pl.ds(pl.multiple_of(start, 8), size)
    state = [(base, rows) for base, rows, _ in plans]
    landing = [base for base, _, _ in plans]
    count = len(plans[0][2])

    def peer(part, step):
        name, stride = plans[part][2][step]
        me = lax.axis_index(name)
        bit = (me // stride) % 2
        return name, me + stride * (1 - 2 * bit), bit

    for step in range(count):
        copies = []
        for part in range(len(plans)):
            name, partner, bit = peer(part, step)
            start, size = state[part]
            half = size // 2
            state[part] = (start + bit * half, half)
            if name in alike:
                continue
            copy = pltpu.make_async_remote_copy(
                src_ref=buf.at[rows_of(start + (1 - bit) * half, half)],
                dst_ref=recv.at[pl.ds(landing[part], half)],
                send_sem=send_sems.at[0, part, step],
                recv_sem=recv_sems.at[0, part, step],
                device_id={name: partner},
                device_id_type=pl.DeviceIdType.MESH,
            )
            copy.start()
            copies.append((part, copy))
        for part, copy in copies:
            copy.wait()
            start, half = state[part]
            mine = rows_of(start, half)
            buf[mine, :] = buf[mine, :] + recv[pl.ds(landing[part], half), :]
            landing[part] += half
    for start, size in state:
        mine = rows_of(start, size)
        out[mine, :] = buf[mine, :]
    for step in reversed(range(count)):
        copies = []
        for part in range(len(plans)):
            name, partner, bit = peer(part, step)
            start, size = state[part]
            mine = rows_of(start, size)
            copy = pltpu.make_async_remote_copy(
                src_ref=out.at[mine],
                dst_ref=out.at[mine],
                send_sem=send_sems.at[1, part, step],
                recv_sem=recv_sems.at[1, part, step],
                device_id={name: partner},
                device_id_type=pl.DeviceIdType.MESH,
            )
            copy.start()
            copies.append(copy)
            state[part] = (start - bit * size, size * 2)
        for copy in copies:
            copy.wait()


def spread_kernel(bits, plans, block_ref, out_ref, buf, recv, send_sems, recv_sems):
    greet(bits)
    buf[...] = block_ref[...]
    sum_over(plans, buf, recv, out_ref, send_sems, recv_sems, alike=("rows",))


def gram_kernel(bits, plans, features_ref, targets_ref, out_ref, buf, recv, send_sems, recv_sems):
    greet(bits)
    tiles = features_ref.shape[0] // LANES
    at = 0
    for i in range(tiles):
        panel = dot_nt(features_ref[i * LANES:(i + 1) * LANES, :], features_ref[:(i + 1) * LANES, :])
        for j in range(i + 1):
            buf[at:at + LANES, :] = panel[:, j * LANES:(j + 1) * LANES]
            at += LANES
    cross = dot_nt(targets_ref[...], features_ref[...])
    depth = cross.shape[0]
    for j in range(tiles):
        buf[at:at + depth, :] = cross[:, j * LANES:(j + 1) * LANES]
        at += depth
    if at < buf.shape[0]:
        buf[at:, :] = jnp.zeros((buf.shape[0] - at, LANES), jnp.float32)
    sum_over(plans, buf, recv, out_ref, send_sems, recv_sems)


def summing_call(kernel, bits, orders, rows, operands, collective_id):
    part_rows = rows // len(orders)
    plans = [(n * part_rows, part_rows, order) for n, order in enumerate(orders)]
    sems = pltpu.SemaphoreType.DMA((2, len(orders), len(bits)))
    return pl.pallas_call(
        functools.partial(kernel, bits, plans),
        out_shape=jax.ShapeDtypeStruct((rows, LANES), jnp.float32),
        in_specs=[pl.BlockSpec(memory_space=pltpu.VMEM)] * len(operands),
        out_specs=pl.BlockSpec(memory_space=pltpu.VMEM),
        scratch_shapes=[
            pltpu.VMEM((rows, LANES), jnp.float32),
            pltpu.VMEM((rows, LANES), jnp.float32),
            sems,
            sems,
        ],
        compiler_params=pltpu.CompilerParams(
            collective_id=collective_id, has_side_effects=True, vmem_limit_bytes=VMEM_LIMIT
        ),
    )(*operands)


def invert(block):
    size = block.shape[0]
    pieces = [block[8 * n:8 * n + 8, :] for n in range(size // 8)]
    lane = lax.broadcasted_iota(jnp.int32, (8, size), 1)
    sub = lax.broadcasted_iota(jnp.int32, (8, size), 0)

    def spread_lane(piece, k):
        return jnp.broadcast_to(piece[:, k:k + 1], (8, size))

    for home in range(size // 8):
        first = 8 * home
        strip = pieces[home]
        square = [spread_lane(strip, first + q) for q in range(8)]
        for q in range(8):
            inverse = 1.0 / jnp.broadcast_to(square[q][q:q + 1, :], (8, size))
            is_row = sub == q
            col = square[q]
            row = jnp.broadcast_to(strip[q:q + 1, :], (8, size)) * inverse
            strip = jnp.where(is_row, row, strip - col * row)
            strip = jnp.where(lane == first + q, jnp.where(is_row, inverse, -col * inverse), strip)
            for m in range(8):
                if m != q:
                    entry = jnp.broadcast_to(square[m][q:q + 1, :], (8, size)) * inverse
                    square[m] = jnp.where(is_row, entry, square[m] - col * entry)
            square[q] = jnp.where(is_row, inverse, -col * inverse)
        factor = jnp.where(lane == first + sub, strip + 1.0, strip)
        rows = [jnp.broadcast_to(factor[q:q + 1, :], (8, size)) for q in range(8)]
        for n in range(size // 8):
            if n != home:
                piece = pieces[n]
                terms = [spread_lane(piece, first + q) * rows[q] for q in range(8)]
                total = ((terms[0] + terms[1]) + (terms[2] + terms[3])) + (
                    (terms[4] + terms[5]) + (terms[6] + terms[7])
                )
                pieces[n] = piece - total
        pieces[home] = strip
    return jnp.concatenate(pieces, axis=0)


def solve_kernel(total_rows, packed_ref, weights_ref, change_ref, panels, diagonal_inverse):
    width = weights_ref.shape[1]
    depth = weights_ref.shape[0]
    tiles = width // LANES
    scale = 1.0 / total_rows
    eye = (
        lax.broadcasted_iota(jnp.int32, (LANES, LANES), 0)
        == lax.broadcasted_iota(jnp.int32, (LANES, LANES), 1)
    )
    at = 0
    for i in range(tiles):
        for j in range(i + 1):
            block = packed_ref[at:at + LANES, :] * scale
            if i == j:
                block = jnp.where(eye, block + penalty, block)
            panels[j, i * LANES:(i + 1) * LANES, :] = block
            at += LANES
    for j in range(tiles):
        panels[j, width:, :] = (
            packed_ref[at:at + depth, :] * scale - penalty * weights_ref[:, j * LANES:(j + 1) * LANES]
        )
        at += depth

    def eliminate(j):
        below = (j + 1) * LANES
        ratio = dot_nn(panels[j, below:, :], diagonal_inverse[...])
        for k in range(j + 1, tiles):
            panels[k, k * LANES:, :] = panels[k, k * LANES:, :] - dot_nt(
                ratio[(k - j - 1) * LANES:, :], panels[j, k * LANES:(k + 1) * LANES, :]
            )
        panels[j, below:, :] = ratio

    def step(j, carry):
        diagonal_inverse[...] = invert(panels[j, pl.ds(pl.multiple_of(j * LANES, LANES), LANES), :])
        for n in range(tiles):
            pl.when(j == n)(functools.partial(eliminate, n))
        return carry

    lax.fori_loop(0, tiles, step, 0)
    for j in reversed(range(tiles)):
        answer = panels[j, width:, :]
        if j + 1 < tiles:
            answer = answer - dot_nn(
                change_ref[:, (j + 1) * LANES:], panels[j, (j + 1) * LANES:width, :]
            )
        change_ref[:, j * LANES:(j + 1) * LANES] = answer


def body(samples, residual, projections, phases, weights, block_order):
    per_device, inputs, width = projections.shape
    classes = residual.shape[1]
    depth = round_up(classes, 8)
    feat_bits = axis_bits("feat", lax.axis_size("feat"))
    rows_bits = axis_bits("rows", lax.axis_size("rows"))
    total_rows = samples.shape[0] * lax.axis_size("rows") * lax.axis_size("feat")
    block_id = block_order[0]
    slot = block_id % per_device
    mine = lax.axis_index("feat") == block_id // per_device

    def local(array):
        block = lax.dynamic_index_in_dim(array, slot, 0, False)
        return jnp.where(mine, block, jnp.zeros_like(block))

    old_weights = lax.psum(local(weights), "feat")
    tiles = width // LANES
    orders = [
        feat_bits + rows_bits,
        feat_bits[:1] + rows_bits + feat_bits[1:],
        feat_bits[:1] + rows_bits[1:] + feat_bits[1:] + rows_bits[:1],
    ]
    bits = feat_bits + rows_bits
    spread_rows = round_up((inputs + 8) * tiles, 8 * 2 ** len(bits) * len(orders))
    basis = jnp.concatenate(
        [local(projections), jnp.broadcast_to(local(phases)[None], (8, width))], axis=0
    ).reshape(-1, LANES)
    basis = jnp.pad(basis, ((0, spread_rows - basis.shape[0]), (0, 0)))
    spread = summing_call(spread_kernel, bits, orders, spread_rows, [basis], 1)
    spread = spread[:(inputs + 8) * tiles].reshape(inputs + 8, width)
    projected = lax.dot_general(
        spread[:inputs], samples, (((0,), (1,)), ((), ())),
        precision=HIGHEST, preferred_element_type=jnp.float32,
    )
    features = root_two * jnp.cos(projected + spread[inputs][:, None])
    targets = jnp.pad(residual.T, ((0, depth - classes), (0, 0)))

    sum_rows = round_up(
        tiles * (tiles + 1) // 2 * LANES + tiles * depth, 8 * 2 ** len(bits) * len(orders)
    )
    packed = summing_call(gram_kernel, bits, orders, sum_rows, [features, targets], 2)

    change = pl.pallas_call(
        functools.partial(solve_kernel, total_rows),
        out_shape=jax.ShapeDtypeStruct((depth, width), jnp.float32),
        in_specs=[pl.BlockSpec(memory_space=pltpu.VMEM)] * 2,
        out_specs=pl.BlockSpec(memory_space=pltpu.VMEM),
        scratch_shapes=[
            pltpu.VMEM((tiles, width + depth, LANES), jnp.float32),
            pltpu.VMEM((LANES, LANES), jnp.float32),
        ],
        compiler_params=pltpu.CompilerParams(vmem_limit_bytes=VMEM_LIMIT),
    )(packed, jnp.pad(old_weights.T, ((0, depth - classes), (0, 0))))[:classes]

    new_weights = old_weights + change.T
    taken = lax.dot_general(
        change, features, (((1,), (0,)), ((), ())), precision=HIGHEST, preferred_element_type=jnp.float32
    )
    return residual - taken.T, new_weights[None]


def solution(mesh):
    return jax.shard_map(
        body,
        mesh=mesh,
        in_specs=(
            P(("rows", "feat"), None),
            P(("rows", "feat"), None),
            P("feat", None, None),
            P("feat", None),
            P("feat", None, None),
            P(),
        ),
        out_specs=(P(("rows", "feat"), None), P()),
        check_vma=False,
    )
```

```python
import functools

import jax
import jax.numpy as jnp
from jax import lax
from jax.experimental import pallas as pl
from jax.experimental.pallas import tpu as pltpu
from jax.sharding import PartitionSpec as P

root_two = 1.4142135623730951
penalty = 0.05
LANES = 128
HIGHEST = lax.Precision.HIGHEST
VMEM_LIMIT = 48 * 1024 * 1024


def round_up(value, step):
    return -(-value // step) * step


def dot_nt(left, right):
    return lax.dot_general(
        left, right, (((1,), (1,)), ((), ())), precision=HIGHEST, preferred_element_type=jnp.float32
    )


def dot_nn(left, right):
    return lax.dot_general(
        left, right, (((1,), (0,)), ((), ())), precision=HIGHEST, preferred_element_type=jnp.float32
    )


def axis_bits(name, size):
    bits, step = [], 1
    while step < size:
        bits.append((name, step))
        step *= 2
    return bits


def greet(bits):
    barrier = pltpu.get_barrier_semaphore()
    for name, step in bits:
        me = lax.axis_index(name)
        partner = me + step * (1 - 2 * ((me // step) % 2))
        pl.semaphore_signal(
            barrier, inc=1, device_id={name: partner}, device_id_type=pl.DeviceIdType.MESH
        )
    pl.semaphore_wait(barrier, len(bits))


def sum_over(plans, buf, recv, out, send_sems, recv_sems, first, alike=()):
    rows_of = lambda start, size: pl.ds(pl.multiple_of(start, 8), size)
    state = [(base, rows) for base, rows, _ in plans]
    landing = [base for base, _, _ in plans]
    count = len(plans[0][2])

    def peer(part, step):
        name, stride = plans[part][2][step]
        me = lax.axis_index(name)
        bit = (me // stride) % 2
        return name, me + stride * (1 - 2 * bit), bit

    def halve(part, step):
        name, partner, bit = peer(part, step)
        start, size = state[part]
        half = size // 2
        state[part] = (start + bit * half, half)
        if name in alike:
            return None
        copy = pltpu.make_async_remote_copy(
            src_ref=buf.at[rows_of(start + (1 - bit) * half, half)],
            dst_ref=recv.at[pl.ds(landing[part], half)],
            send_sem=send_sems.at[0, part, step],
            recv_sem=recv_sems.at[0, part, step],
            device_id={name: partner},
            device_id_type=pl.DeviceIdType.MESH,
        )
        copy.start()
        return copy

    def double(part, step):
        name, partner, bit = peer(part, step)
        start, size = state[part]
        mine = rows_of(start, size)
        copy = pltpu.make_async_remote_copy(
            src_ref=out.at[mine],
            dst_ref=out.at[mine],
            send_sem=send_sems.at[1, part, step],
            recv_sem=recv_sems.at[1, part, step],
            device_id={name: partner},
            device_id_type=pl.DeviceIdType.MESH,
        )
        copy.start()
        state[part] = (start - bit * size, size * 2)
        return copy

    def finish(part, step, copy):
        if copy is None:
            return
        copy.wait()
        start, half = state[part]
        mine = rows_of(start, half)
        buf[mine, :] = buf[mine, :] + recv[pl.ds(landing[part], half), :]
        landing[part] += half

    parts = range(len(plans))
    copies = [first(part, lambda part=part: halve(part, 0)) for part in parts]
    for step in range(count):
        for part in parts:
            finish(part, step, copies[part])
            if step + 1 < count:
                copies[part] = halve(part, step + 1)
            else:
                start, size = state[part]
                mine = rows_of(start, size)
                out[mine, :] = buf[mine, :]
                copies[part] = double(part, count - 1)
    for step in reversed(range(count)):
        for part in parts:
            copies[part].wait()
            if step > 0:
                copies[part] = double(part, step - 1)


def spread_kernel(bits, plans, block_ref, out_ref, buf, recv, send_sems, recv_sems):
    greet(bits)
    buf[...] = block_ref[...]
    sum_over(plans, buf, recv, out_ref, send_sems, recv_sems, lambda part, go: go(), alike=("rows",))


def gram_kernel(bits, plans, features_ref, targets_ref, pull_ref, out_ref, buf, recv, send_sems, recv_sems):
    greet(bits)
    tiles = features_ref.shape[0] // LANES
    depth = targets_ref.shape[0]
    done = [0, 0]

    def fill(part, go):
        end = plans[part][0] + plans[part][1]
        while done[0] < end:
            i, at = done[1], done[0]
            if i < tiles:
                panel = dot_nt(
                    features_ref[i * LANES:(i + 1) * LANES, :], features_ref[:(i + 1) * LANES, :]
                )
                for j in range(i + 1):
                    buf[at:at + LANES, :] = panel[:, j * LANES:(j + 1) * LANES]
                    at += LANES
            elif i == tiles:
                cross = dot_nt(targets_ref[...], features_ref[...]) + pull_ref[...]
                for j in range(tiles):
                    buf[at:at + depth, :] = cross[:, j * LANES:(j + 1) * LANES]
                    at += depth
            else:
                buf[at:, :] = jnp.zeros((buf.shape[0] - at, LANES), jnp.float32)
                at = buf.shape[0]
            done[:] = [at, i + 1]
        return go()

    sum_over(plans, buf, recv, out_ref, send_sems, recv_sems, fill)


def summing_call(kernel, bits, orders, rows, operands, collective_id):
    part_rows = rows // len(orders)
    plans = [(n * part_rows, part_rows, order) for n, order in enumerate(orders)]
    sems = pltpu.SemaphoreType.DMA((2, len(orders), len(bits)))
    return pl.pallas_call(
        functools.partial(kernel, bits, plans),
        out_shape=jax.ShapeDtypeStruct((rows, LANES), jnp.float32),
        in_specs=[pl.BlockSpec(memory_space=pltpu.VMEM)] * len(operands),
        out_specs=pl.BlockSpec(memory_space=pltpu.VMEM),
        scratch_shapes=[
            pltpu.VMEM((rows, LANES), jnp.float32),
            pltpu.VMEM((rows, LANES), jnp.float32),
            sems,
            sems,
        ],
        compiler_params=pltpu.CompilerParams(
            collective_id=collective_id, has_side_effects=True, vmem_limit_bytes=VMEM_LIMIT
        ),
    )(*operands)


def invert(block):
    size = block.shape[0]
    pieces = [block[8 * n:8 * n + 8, :] for n in range(size // 8)]
    lane = lax.broadcasted_iota(jnp.int32, (8, size), 1)
    sub = lax.broadcasted_iota(jnp.int32, (8, size), 0)

    def spread_lane(piece, k):
        return jnp.broadcast_to(piece[:, k:k + 1], (8, size))

    for home in range(size // 8):
        first = 8 * home
        strip = pieces[home]
        square = [spread_lane(strip, first + q) for q in range(8)]
        for q in range(8):
            inverse = 1.0 / jnp.broadcast_to(square[q][q:q + 1, :], (8, size))
            is_row = sub == q
            col = square[q]
            row = jnp.broadcast_to(strip[q:q + 1, :], (8, size)) * inverse
            strip = jnp.where(is_row, row, strip - col * row)
            strip = jnp.where(lane == first + q, jnp.where(is_row, inverse, -col * inverse), strip)
            for m in range(8):
                if m != q:
                    entry = jnp.broadcast_to(square[m][q:q + 1, :], (8, size)) * inverse
                    square[m] = jnp.where(is_row, entry, square[m] - col * entry)
            square[q] = jnp.where(is_row, inverse, -col * inverse)
        factor = jnp.where(lane == first + sub, strip + 1.0, strip)
        rows = [jnp.broadcast_to(factor[q:q + 1, :], (8, size)) for q in range(8)]
        for n in range(size // 8):
            if n != home:
                piece = pieces[n]
                terms = [spread_lane(piece, first + q) * rows[q] for q in range(8)]
                total = ((terms[0] + terms[1]) + (terms[2] + terms[3])) + (
                    (terms[4] + terms[5]) + (terms[6] + terms[7])
                )
                pieces[n] = piece - total
        pieces[home] = strip
    return jnp.concatenate(pieces, axis=0)


def solve_kernel(total_rows, packed_ref, change_ref, panels, diagonal_inverse):
    depth, width = change_ref.shape
    tiles = width // LANES
    scale = 1.0 / total_rows
    eye = (
        lax.broadcasted_iota(jnp.int32, (LANES, LANES), 0)
        == lax.broadcasted_iota(jnp.int32, (LANES, LANES), 1)
    )
    at = 0
    for i in range(tiles):
        for j in range(i + 1):
            block = packed_ref[at:at + LANES, :] * scale
            if i == j:
                block = jnp.where(eye, block + penalty, block)
            panels[j, i * LANES:(i + 1) * LANES, :] = block
            at += LANES
    for j in range(tiles):
        panels[j, width:, :] = packed_ref[at:at + depth, :] * scale
        at += depth

    def eliminate(j):
        below = (j + 1) * LANES
        ratio = dot_nn(panels[j, below:, :], diagonal_inverse[...])
        for k in range(j + 1, tiles):
            panels[k, k * LANES:, :] = panels[k, k * LANES:, :] - dot_nt(
                ratio[(k - j - 1) * LANES:, :], panels[j, k * LANES:(k + 1) * LANES, :]
            )
        panels[j, below:, :] = ratio

    def step(j, carry):
        diagonal_inverse[...] = invert(panels[j, pl.ds(pl.multiple_of(j * LANES, LANES), LANES), :])
        for n in range(tiles):
            pl.when(j == n)(functools.partial(eliminate, n))
        return carry

    lax.fori_loop(0, tiles, step, 0)
    for j in reversed(range(tiles)):
        answer = panels[j, width:, :]
        if j + 1 < tiles:
            answer = answer - dot_nn(
                change_ref[:, (j + 1) * LANES:], panels[j, (j + 1) * LANES:width, :]
            )
        change_ref[:, j * LANES:(j + 1) * LANES] = answer


def body(samples, residual, projections, phases, weights, block_order):
    per_device, inputs, width = projections.shape
    classes = residual.shape[1]
    depth = round_up(classes, 8)
    feat_bits = axis_bits("feat", lax.axis_size("feat"))
    rows_bits = axis_bits("rows", lax.axis_size("rows"))
    total_rows = samples.shape[0] * lax.axis_size("rows") * lax.axis_size("feat")
    block_id = block_order[0]
    slot = block_id % per_device
    mine = lax.axis_index("feat") == block_id // per_device

    def local(array):
        block = lax.dynamic_index_in_dim(array, slot, 0, False)
        return jnp.where(mine, block, jnp.zeros_like(block))

    own_weights = local(weights)
    tiles = width // LANES
    orders = [
        feat_bits + rows_bits,
        feat_bits[:1] + rows_bits + feat_bits[1:],
        feat_bits[:1] + rows_bits[1:] + feat_bits[1:] + rows_bits[:1],
    ]
    bits = feat_bits + rows_bits
    spread_rows = round_up((inputs + 8) * tiles, 8 * 2 ** len(bits) * len(orders))
    basis = jnp.concatenate(
        [local(projections), jnp.broadcast_to(local(phases)[None], (8, width))], axis=0
    ).reshape(-1, LANES)
    basis = jnp.pad(basis, ((0, spread_rows - basis.shape[0]), (0, 0)))
    spread = summing_call(spread_kernel, bits, orders, spread_rows, [basis], 1)
    spread = spread[:(inputs + 8) * tiles].reshape(inputs + 8, width)
    projected = lax.dot_general(
        spread[:inputs], samples, (((0,), (1,)), ((), ())),
        precision=HIGHEST, preferred_element_type=jnp.float32,
    )
    features = root_two * jnp.cos(projected + spread[inputs][:, None])
    targets = jnp.pad(residual.T, ((0, depth - classes), (0, 0)))

    orders = orders * 2
    pull = jnp.where(lax.axis_index("rows") == 0, -penalty * total_rows * own_weights.T, 0.0)
    pull = jnp.pad(pull, ((0, depth - classes), (0, 0)))
    sum_rows = round_up(
        tiles * (tiles + 1) // 2 * LANES + tiles * depth, 8 * 2 ** len(bits) * len(orders)
    )
    packed = summing_call(gram_kernel, bits, orders, sum_rows, [features, targets, pull], 2)
    own_weights, packed = lax.optimization_barrier((own_weights, packed))
    old_weights = lax.psum(own_weights, "feat")

    change = pl.pallas_call(
        functools.partial(solve_kernel, total_rows),
        out_shape=jax.ShapeDtypeStruct((depth, width), jnp.float32),
        in_specs=[pl.BlockSpec(memory_space=pltpu.VMEM)],
        out_specs=pl.BlockSpec(memory_space=pltpu.VMEM),
        scratch_shapes=[
            pltpu.VMEM((tiles, width + depth, LANES), jnp.float32),
            pltpu.VMEM((LANES, LANES), jnp.float32),
        ],
        compiler_params=pltpu.CompilerParams(vmem_limit_bytes=VMEM_LIMIT),
        cost_estimate=pl.CostEstimate(
            flops=12 * width * width * (width // 3 + depth), bytes_accessed=2 * packed.size * 4, transcendentals=0
        ),
    )(packed)[:classes]

    new_weights = old_weights + change.T
    taken = lax.dot_general(
        change, features, (((1,), (0,)), ((), ())), precision=HIGHEST, preferred_element_type=jnp.float32
    )
    return residual - taken.T, new_weights[None]


def solution(mesh):
    return jax.shard_map(
        body,
        mesh=mesh,
        in_specs=(
            P(("rows", "feat"), None),
            P(("rows", "feat"), None),
            P("feat", None, None),
            P("feat", None),
            P("feat", None, None),
            P(),
        ),
        out_specs=(P(("rows", "feat"), None), P()),
        check_vma=False,
    )
```

```python
import functools

import jax
import jax.numpy as jnp
from jax import lax
from jax.experimental import pallas as pl
from jax.experimental.pallas import tpu as pltpu
from jax.sharding import PartitionSpec as P

root_two = 1.4142135623730951
penalty = 0.05
LANES = 128
HIGHEST = lax.Precision.HIGHEST
VMEM_LIMIT = 48 * 1024 * 1024


def round_up(value, step):
    return -(-value // step) * step


def dot_nt(left, right):
    return lax.dot_general(
        left, right, (((1,), (1,)), ((), ())), precision=HIGHEST, preferred_element_type=jnp.float32
    )


def dot_nn(left, right):
    return lax.dot_general(
        left, right, (((1,), (0,)), ((), ())), precision=HIGHEST, preferred_element_type=jnp.float32
    )


def axis_bits(name, size):
    bits, step = [], 1
    while step < size:
        bits.append((name, step))
        step *= 2
    return bits


def greet(bits):
    barrier = pltpu.get_barrier_semaphore()
    for name, step in bits:
        me = lax.axis_index(name)
        partner = me + step * (1 - 2 * ((me // step) % 2))
        pl.semaphore_signal(
            barrier, inc=1, device_id={name: partner}, device_id_type=pl.DeviceIdType.MESH
        )
    pl.semaphore_wait(barrier, len(bits))


def sum_over(plans, buf, recv, out, send_sems, recv_sems, first, alike=()):
    rows_of = lambda start, size: pl.ds(pl.multiple_of(start, 8), size)
    state = [(base, rows) for base, rows, _ in plans]
    landing = [base for base, _, _ in plans]
    count = len(plans[0][2])

    def peer(part, step):
        name, stride = plans[part][2][step]
        me = lax.axis_index(name)
        bit = (me // stride) % 2
        return name, me + stride * (1 - 2 * bit), bit

    def halve(part, step):
        name, partner, bit = peer(part, step)
        start, size = state[part]
        half = size // 2
        state[part] = (start + bit * half, half)
        if name in alike:
            return None
        copy = pltpu.make_async_remote_copy(
            src_ref=buf.at[rows_of(start + (1 - bit) * half, half)],
            dst_ref=recv.at[pl.ds(landing[part], half)],
            send_sem=send_sems.at[0, part, step],
            recv_sem=recv_sems.at[0, part, step],
            device_id={name: partner},
            device_id_type=pl.DeviceIdType.MESH,
        )
        copy.start()
        return copy

    def double(part, step):
        name, partner, bit = peer(part, step)
        start, size = state[part]
        mine = rows_of(start, size)
        copy = pltpu.make_async_remote_copy(
            src_ref=out.at[mine],
            dst_ref=out.at[mine],
            send_sem=send_sems.at[1, part, step],
            recv_sem=recv_sems.at[1, part, step],
            device_id={name: partner},
            device_id_type=pl.DeviceIdType.MESH,
        )
        copy.start()
        state[part] = (start - bit * size, size * 2)
        return copy

    def finish(part, step, copy):
        if copy is None:
            return
        copy.wait()
        start, half = state[part]
        mine = rows_of(start, half)
        buf[mine, :] = buf[mine, :] + recv[pl.ds(landing[part], half), :]
        landing[part] += half

    parts = range(len(plans))
    copies = [first(part, lambda part=part: halve(part, 0)) for part in parts]
    for step in range(count):
        for part in parts:
            finish(part, step, copies[part])
            if step + 1 < count:
                copies[part] = halve(part, step + 1)
            else:
                start, size = state[part]
                mine = rows_of(start, size)
                out[mine, :] = buf[mine, :]
                copies[part] = double(part, count - 1)
    for step in reversed(range(count)):
        for part in parts:
            copies[part].wait()
            if step > 0:
                copies[part] = double(part, step - 1)


def spread_kernel(bits, plans, block_ref, out_ref, buf, recv, send_sems, recv_sems):
    greet(bits)
    buf[...] = block_ref[...]
    sum_over(plans, buf, recv, out_ref, send_sems, recv_sems, lambda part, go: go(), alike=("rows",))


def gram_kernel(bits, plans, features_ref, targets_ref, pull_ref, out_ref, buf, recv, send_sems, recv_sems):
    greet(bits)
    tiles = features_ref.shape[0] // LANES
    depth = targets_ref.shape[0]
    done = [0, 0]

    def fill(part, go):
        end = plans[part][0] + plans[part][1]
        while done[0] < end:
            i, at = done[1], done[0]
            if i < tiles:
                panel = dot_nt(
                    features_ref[i * LANES:(i + 1) * LANES, :], features_ref[:(i + 1) * LANES, :]
                )
                for j in range(i + 1):
                    buf[at:at + LANES, :] = panel[:, j * LANES:(j + 1) * LANES]
                    at += LANES
            elif i == tiles:
                cross = dot_nt(targets_ref[...], features_ref[...]) + pull_ref[...]
                for j in range(tiles):
                    buf[at:at + depth, :] = cross[:, j * LANES:(j + 1) * LANES]
                    at += depth
            else:
                buf[at:, :] = jnp.zeros((buf.shape[0] - at, LANES), jnp.float32)
                at = buf.shape[0]
            done[:] = [at, i + 1]
        return go()

    sum_over(plans, buf, recv, out_ref, send_sems, recv_sems, fill)


def summing_call(kernel, bits, orders, rows, operands, collective_id):
    part_rows = rows // len(orders)
    plans = [(n * part_rows, part_rows, order) for n, order in enumerate(orders)]
    sems = pltpu.SemaphoreType.DMA((2, len(orders), len(bits)))
    return pl.pallas_call(
        functools.partial(kernel, bits, plans),
        out_shape=jax.ShapeDtypeStruct((rows, LANES), jnp.float32),
        in_specs=[pl.BlockSpec(memory_space=pltpu.VMEM)] * len(operands),
        out_specs=pl.BlockSpec(memory_space=pltpu.VMEM),
        scratch_shapes=[
            pltpu.VMEM((rows, LANES), jnp.float32),
            pltpu.VMEM((rows, LANES), jnp.float32),
            sems,
            sems,
        ],
        compiler_params=pltpu.CompilerParams(
            collective_id=collective_id, has_side_effects=True, vmem_limit_bytes=VMEM_LIMIT
        ),
    )(*operands)


def invert(block):
    size = block.shape[0]
    pieces = [block[8 * n:8 * n + 8, :] for n in range(size // 8)]
    lane = lax.broadcasted_iota(jnp.int32, (8, size), 1)
    sub = lax.broadcasted_iota(jnp.int32, (8, size), 0)

    def spread_lane(piece, k):
        return jnp.broadcast_to(piece[:, k:k + 1], (8, size))

    for home in range(size // 8):
        first = 8 * home
        strip = pieces[home]
        square = [spread_lane(strip, first + q) for q in range(8)]
        for q in range(8):
            inverse = 1.0 / jnp.broadcast_to(square[q][q:q + 1, :], (8, size))
            is_row = sub == q
            col = square[q]
            row = jnp.broadcast_to(strip[q:q + 1, :], (8, size)) * inverse
            strip = jnp.where(is_row, row, strip - col * row)
            strip = jnp.where(lane == first + q, jnp.where(is_row, inverse, -col * inverse), strip)
            for m in range(8):
                if m != q:
                    entry = jnp.broadcast_to(square[m][q:q + 1, :], (8, size)) * inverse
                    square[m] = jnp.where(is_row, entry, square[m] - col * entry)
            square[q] = jnp.where(is_row, inverse, -col * inverse)
        factor = jnp.where(lane == first + sub, strip + 1.0, strip)
        rows = [jnp.broadcast_to(factor[q:q + 1, :], (8, size)) for q in range(8)]
        for n in range(size // 8):
            if n != home:
                piece = pieces[n]
                terms = [spread_lane(piece, first + q) * rows[q] for q in range(8)]
                total = ((terms[0] + terms[1]) + (terms[2] + terms[3])) + (
                    (terms[4] + terms[5]) + (terms[6] + terms[7])
                )
                pieces[n] = piece - total
        pieces[home] = strip
    return jnp.concatenate(pieces, axis=0)


def solve_kernel(total_rows, packed_ref, change_ref, panels, diagonal_inverse):
    depth, width = change_ref.shape
    tiles = width // LANES
    scale = 1.0 / total_rows
    eye = (
        lax.broadcasted_iota(jnp.int32, (LANES, LANES), 0)
        == lax.broadcasted_iota(jnp.int32, (LANES, LANES), 1)
    )
    at = 0
    for i in range(tiles):
        for j in range(i + 1):
            block = packed_ref[at:at + LANES, :] * scale
            if i == j:
                block = jnp.where(eye, block + penalty, block)
            panels[j, i * LANES:(i + 1) * LANES, :] = block
            at += LANES
    for j in range(tiles):
        panels[j, width:, :] = packed_ref[at:at + depth, :] * scale
        at += depth

    def eliminate(j):
        below = (j + 1) * LANES
        ratio = dot_nn(panels[j, below:, :], diagonal_inverse[...])
        for k in range(j + 1, tiles, 2):
            last = min(k + 2, tiles)
            delta = dot_nt(ratio[(k - j - 1) * LANES:, :], panels[j, k * LANES:last * LANES, :])
            for n in range(k, last):
                skip = (n - k) * LANES
                panels[n, n * LANES:, :] = panels[n, n * LANES:, :] - delta[skip:, skip:skip + LANES]
        panels[j, below:, :] = ratio

    def step(j, carry):
        diagonal_inverse[...] = invert(panels[j, pl.ds(pl.multiple_of(j * LANES, LANES), LANES), :])
        for n in range(tiles):
            pl.when(j == n)(functools.partial(eliminate, n))
        return carry

    lax.fori_loop(0, tiles, step, 0)
    for j in reversed(range(tiles)):
        answer = panels[j, width:, :]
        if j + 1 < tiles:
            answer = answer - dot_nn(
                change_ref[:, (j + 1) * LANES:], panels[j, (j + 1) * LANES:width, :]
            )
        change_ref[:, j * LANES:(j + 1) * LANES] = answer


def body(samples, residual, projections, phases, weights, block_order):
    per_device, inputs, width = projections.shape
    classes = residual.shape[1]
    depth = round_up(classes, 8)
    feat_bits = axis_bits("feat", lax.axis_size("feat"))
    rows_bits = axis_bits("rows", lax.axis_size("rows"))
    total_rows = samples.shape[0] * lax.axis_size("rows") * lax.axis_size("feat")
    block_id = block_order[0]
    slot = block_id % per_device
    mine = lax.axis_index("feat") == block_id // per_device

    def local(array):
        block = lax.dynamic_index_in_dim(array, slot, 0, False)
        return jnp.where(mine, block, jnp.zeros_like(block))

    own_weights = local(weights)
    tiles = width // LANES
    orders = [
        feat_bits + rows_bits,
        feat_bits[:1] + rows_bits + feat_bits[1:],
        feat_bits[:1] + rows_bits[1:] + feat_bits[1:] + rows_bits[:1],
    ]
    bits = feat_bits + rows_bits
    spread_rows = round_up((inputs + 8) * tiles, 8 * 2 ** len(bits) * len(orders))
    basis = jnp.concatenate(
        [local(projections), jnp.broadcast_to(local(phases)[None], (8, width))], axis=0
    ).reshape(-1, LANES)
    basis = jnp.pad(basis, ((0, spread_rows - basis.shape[0]), (0, 0)))
    spread = summing_call(spread_kernel, bits, orders, spread_rows, [basis], 1)
    spread = spread[:(inputs + 8) * tiles].reshape(inputs + 8, width)
    projected = lax.dot_general(
        spread[:inputs], samples, (((0,), (1,)), ((), ())),
        precision=HIGHEST, preferred_element_type=jnp.float32,
    )
    features = root_two * jnp.cos(projected + spread[inputs][:, None])
    targets = jnp.pad(residual.T, ((0, depth - classes), (0, 0)))

    orders = orders * 2
    pull = jnp.where(lax.axis_index("rows") == 0, -penalty * total_rows * own_weights.T, 0.0)
    pull = jnp.pad(pull, ((0, depth - classes), (0, 0)))
    sum_rows = round_up(
        tiles * (tiles + 1) // 2 * LANES + tiles * depth, 8 * 2 ** len(bits) * len(orders)
    )
    packed = summing_call(gram_kernel, bits, orders, sum_rows, [features, targets, pull], 2)
    own_weights, packed = lax.optimization_barrier((own_weights, packed))
    old_weights = lax.psum(own_weights, "feat")

    change = pl.pallas_call(
        functools.partial(solve_kernel, total_rows),
        out_shape=jax.ShapeDtypeStruct((depth, width), jnp.float32),
        in_specs=[pl.BlockSpec(memory_space=pltpu.VMEM)],
        out_specs=pl.BlockSpec(memory_space=pltpu.VMEM),
        scratch_shapes=[
            pltpu.VMEM((tiles, width + depth, LANES), jnp.float32),
            pltpu.VMEM((LANES, LANES), jnp.float32),
        ],
        compiler_params=pltpu.CompilerParams(vmem_limit_bytes=VMEM_LIMIT),
        cost_estimate=pl.CostEstimate(
            flops=12 * width * width * (width // 3 + depth), bytes_accessed=2 * packed.size * 4, transcendentals=0
        ),
    )(packed)[:classes]

    new_weights = old_weights + change.T
    taken = lax.dot_general(
        change, features, (((1,), (0,)), ((), ())), precision=HIGHEST, preferred_element_type=jnp.float32
    )
    return residual - taken.T, new_weights[None]


def solution(mesh):
    return jax.shard_map(
        body,
        mesh=mesh,
        in_specs=(
            P(("rows", "feat"), None),
            P(("rows", "feat"), None),
            P("feat", None, None),
            P("feat", None),
            P("feat", None, None),
            P(),
        ),
        out_specs=(P(("rows", "feat"), None), P()),
        check_vma=False,
    )
```
